32 devices in a mesh: team: 8 (over y, x, core), rep: 4 (over z).
Axes of the slice: x: 2, y: 2, z: 4, core: 2. Of those that a mesh axis runs over, the one named last changes fastest.
Arguments:
- features: bfloat16 [1024, 1024], P(('team', 'rep')), may hold values from -6 to 6
- degree: int32 [1024], P(('team', 'rep')), may hold values from 4 to 16
- blocks: bfloat16 [8, 4, 2, 128, 128], P('team', 'rep'), may hold values from -3 to 3
- block_cols: int32 [8, 4, 2], P('team', 'rep'), may hold values from 0 to 1, each once within a row
- block_count: int32 [8, 4], P('team', 'rep'), may hold values from 1 to 2, as said below
Outputs:
- hop1: bfloat16 [1024, 1024], P(('team', 'rep'))
- hop2: bfloat16 [1024, 1024], P(('team', 'rep'))
- hop3: bfloat16 [1024, 1024], P(('team', 'rep'))
The draws below stay inside these ranges and needn't reach their ends.
Inputs may be any that keep to these rules, and one draw needn't show every extreme that they name: Each of the 2 entries of a row of block_cols names a different column block; only the first block_count entries are used. `block_count`: some block row of some replica uses all 2 of its blocks.
All inputs are finite; a program needn't handle non-finite values.
Results may differ from the reference program's by a relative error of at most 0.04.
Values may be sent and summed in bfloat16 or wider, within the bound.
A program may use at most 64 MiB of HBM per device.

```python
import jax
import jax.numpy as jnp
from jax import lax

F = 1024
BLK = 128
HOPS = 3
ROWS = 32
NODES = 1024
NBR = 8
CBLK = 2
N_TEAM = 8
N_REP = 4


def draw_block_count(key, part):
    first, second, third = jax.random.split(key, 3)
    left = jax.random.randint(first, (NBR, N_REP), 1, CBLK + 1)
    right = jax.random.randint(second, (NBR, N_REP), 1, CBLK + 1)
    counts = jnp.minimum(left, right).reshape(-1)
    chosen = jax.random.randint(third, (), 0, NBR * N_REP)
    counts = counts.at[chosen].set(CBLK)
    return counts.reshape(NBR, N_REP).astype(jnp.int32)


def place_ends(entries, stream_key, least, top_value):
    index_at = [jax.random.randint(jax.random.fold_in(stream_key, axis), (), 0, length) for axis, length in enumerate(entries.shape)]
    main_axis = entries.shape.index(max(entries.shape))
    beside = index_at[:main_axis] + [(index_at[main_axis] + 1) % entries.shape[main_axis]] + index_at[main_axis + 1:]
    return entries.at[tuple(index_at)].set(least).at[tuple(beside)].set(top_value)


def steps_of(own_key, dims, cuts, smallest, top_value):
    def one(dim, shards_of):
        draws = jax.random.uniform(jax.random.fold_in(jax.random.fold_in(own_key, 6), dim), (shards_of,), jnp.float32, smallest / len(cuts), top_value / len(cuts))
        return jnp.repeat(jnp.exp(draws), dims[dim] // shards_of).reshape((-1,) + (1,) * (len(dims) - dim - 1))

    factor_of = one(*cuts[0])
    for cut in cuts[1:]:
        factor_of = factor_of * one(*cut)
    return factor_of


def noise(rng, extent, width, limit, pieces=(), kind=jnp.bfloat16):
    values = jax.random.normal(rng, extent, jnp.float32) * width
    if len(pieces) > 0:
        values = steps_of(rng, extent, pieces, -0.22, 0.18) * values
    return jnp.clip(values, min=-limit, max=limit).astype(kind)


def setup_inputs(seed: int = 0) -> dict:
    seeds = jax.random.split(jax.random.key(seed), 6)
    features = noise(seeds[0], (NODES, F), 1.0, 6.0, ((0, 32),))
    degree = place_ends(jax.random.randint(seeds[1], (NODES,), 4, 17), jax.random.fold_in(seeds[1], 1), 4, 16).astype(jnp.int32)
    blocks = noise(seeds[2], (NBR, N_REP, CBLK, BLK, BLK), 0.5, 3.0, ((0, 8), (1, 4)))
    block_cols = jax.vmap(lambda own: jax.random.permutation(own, CBLK))(jax.random.split(seeds[3], NBR * N_REP)).reshape((NBR, N_REP, CBLK)).astype(jnp.int32)
    block_count = draw_block_count(jax.random.fold_in(seeds[5], 71), 0)
    return {"features": features, "degree": degree, "blocks": blocks, "block_cols": block_cols, "block_count": block_count}


def reference(features, degree, blocks, block_cols, block_count):
    scale = lax.rsqrt(degree.astype(jnp.float32))[:, None]
    slots = jnp.arange(CBLK)
    picks = (block_cols[..., None] == slots[None, None, None, :]) & (slots[None, None, :, None] < block_count[:, :, None, None])
    picks = picks.astype(jnp.float32)
    current = features
    results = []
    for hop in range(HOPS):
        sent = (scale * current.astype(jnp.float32)).astype(jnp.bfloat16)
        sent = lax.optimization_barrier(sent)
        sent_wide = sent.astype(jnp.float32)
        grouped = sent_wide.reshape(N_TEAM, N_REP, ROWS, F)

        def add_replica(replica, total):
            columns = lax.dynamic_index_in_dim(grouped, replica, 1, keepdims=False).reshape(N_TEAM * ROWS, F)
            tiles = lax.dynamic_index_in_dim(blocks, replica, 1, keepdims=False).astype(jnp.float32)
            chosen = lax.dynamic_index_in_dim(picks, replica, 1, keepdims=False)
            dense = jnp.einsum('gtuv,gtb->gubv', tiles, chosen, precision=lax.Precision.HIGHEST)
            dense = dense.reshape(NODES, CBLK * BLK)
            partial_value = jnp.dot(dense, columns, precision=lax.Precision.HIGHEST, preferred_element_type=jnp.float32)
            partial_value = lax.optimization_barrier(partial_value.astype(jnp.bfloat16)).astype(jnp.float32)
            return total + partial_value
        total = lax.fori_loop(0, N_REP, add_replica, jnp.zeros((NODES, F), jnp.float32))
        current = (scale * (total + sent_wide)).astype(jnp.bfloat16)
        results.append(current)
    return (results[0], results[1], results[2])
```

```python
import functools

import jax
import jax.numpy as jnp
from jax import lax
from jax.experimental import pallas as pl
from jax.experimental.pallas import tpu as pltpu
from jax.sharding import PartitionSpec as P

HOPS = 3
PAIR = 2
LANES = 128
MESH_IDS = pl.DeviceIdType.MESH


def diffuse_kernel(n_team, n_rep, features, degree, blocks, block_cols, block_count,
                   out1, out2, out3, sent, gathered, adjacency, scales, hops,
                   feat_send, feat_recv, scale_send, scale_recv, adj_send, adj_recv,
                   pass_send, pass_recv, hop_send, hop_recv, out_send, out_recv):
    groups = n_rep * PAIR
    chips = n_team // PAIR
    rows, width = features.shape
    group_width = width // groups
    slots, block_size = blocks.shape[2], blocks.shape[-1]
    panel = n_rep * rows
    team, rep = lax.axis_index("team"), lax.axis_index("rep")
    chip, core = team // PAIR, lax.rem(team, PAIR)
    group = rep * PAIR + core
    outs = (out1, out2, out3)

    def column_peer(step):
        other = lax.rem(group + step, groups)
        return other, (chip * PAIR + lax.rem(other, PAIR), other // PAIR)

    def plane_peer(step):
        return (lax.rem(chip + step, chips) * PAIR + core, rep)

    def remote(src, dst, send_sem, recv_sem, device):
        return pltpu.make_async_remote_copy(
            src_ref=src, dst_ref=dst, send_sem=send_sem, recv_sem=recv_sem,
            device_id=device, device_id_type=MESH_IDS)

    barrier = pltpu.get_barrier_semaphore()
    for step in range(1, groups):
        pl.semaphore_signal(barrier, inc=1, device_id=column_peer(step)[1], device_id_type=MESH_IDS)
    for step in range(1, chips):
        pl.semaphore_signal(barrier, inc=1, device_id=plane_peer(step), device_id_type=MESH_IDS)

    own_scale = lax.rsqrt(degree[...].astype(jnp.float32))

    def as_column(row):
        on_diagonal = (lax.broadcasted_iota(jnp.int32, (rows, rows), 0)
                       == lax.broadcasted_iota(jnp.int32, (rows, rows), 1))
        spread = jnp.where(on_diagonal, jnp.broadcast_to(row, (rows, rows)), 0.0)
        return jnp.sum(spread, axis=1, keepdims=True)

    own_column = as_column(own_scale)
    for index in range(groups):
        part = features[:, index * group_width:(index + 1) * group_width].astype(jnp.float32)
        sent[index] = (own_column * part).astype(jnp.bfloat16)
    scales[core, rep, 0:1, 0:rows] = own_scale

    for column in range(n_team * rows // block_size):
        dense = jnp.zeros((block_size, block_size), jnp.float32)
        for slot in range(slots):
            used = (block_cols[0, 0, slot] == column) & (slot < block_count[0, 0])
            factor = jnp.where(used, 1.0, 0.0).astype(jnp.float32)
            dense = dense + factor * blocks[0, 0, slot].astype(jnp.float32)
        adjacency[rep, core, :, column * block_size:(column + 1) * block_size] = dense.astype(jnp.bfloat16)

    pl.semaphore_wait(barrier, groups - 1 + chips - 1)

    feature_copies, scale_copies, adjacency_copies, pass_copies = [], [], [], []
    for step in range(1, groups):
        other, device = column_peer(step)
        copy = remote(sent.at[other], gathered.at[0, rep, team],
                      feat_send.at[step - 1], feat_recv.at[step - 1], device)
        copy.start()
        feature_copies.append(copy)
    sibling = (chip * PAIR + lax.rem(core + 1, PAIR), rep)
    copy = remote(adjacency.at[rep, core], adjacency.at[rep, core],
                  pass_send.at[0], pass_recv.at[0], sibling)
    copy.start()
    pass_copies.append(copy)
    for step in range(1, n_rep):
        copy = remote(adjacency.at[rep, core], adjacency.at[rep, core],
                      adj_send.at[step - 1], adj_recv.at[step - 1],
                      (team, lax.rem(rep + step, n_rep)))
        copy.start()
        adjacency_copies.append(copy)
    for step in range(1, groups):
        copy = remote(scales.at[core, rep], scales.at[core, rep],
                      scale_send.at[step - 1], scale_recv.at[step - 1], column_peer(step)[1])
        copy.start()
        scale_copies.append(copy)
    gathered[0, rep, team] = sent[group]

    def send_hop(hop):
        copies = []
        for step in range(1, chips):
            own = gathered.at[hop, :, pl.ds(chip * PAIR, PAIR)]
            copy = remote(own, own, hop_send.at[hop, step - 1], hop_recv.at[hop, step - 1],
                          plane_peer(step))
            copy.start()
            copies.append(copy)
        return copies

    for copy in feature_copies:
        copy.wait_recv()
    hop_copies = [send_hop(0)]

    for step in range(1, n_rep):
        adjacency_copies[step - 1].wait_recv()
        source = lax.rem(rep + n_rep - step, n_rep)
        copy = remote(adjacency.at[source, core], adjacency.at[source, core],
                      pass_send.at[step], pass_recv.at[step], sibling)
        copy.start()
        pass_copies.append(copy)
    for copy in scale_copies:
        copy.wait_recv()
    scale_column = jnp.concatenate(
        [as_column(scales[c, r, 0:1, 0:rows]) for c in range(PAIR) for r in range(n_rep)], axis=0)
    for copy in pass_copies:
        copy.wait_recv()

    out_copies = []
    for hop in range(HOPS):
        for copy in hop_copies[hop]:
            copy.wait_recv()
        total = jnp.concatenate(
            [gathered[hop, :, chip * PAIR + c].reshape(panel, group_width) for c in range(PAIR)],
            axis=0).astype(jnp.float32)
        for r in range(n_rep):
            total = total + jnp.dot(
                adjacency[r].reshape(PAIR * panel, n_team * rows),
                gathered[hop, r].reshape(n_team * rows, group_width),
                preferred_element_type=jnp.float32)
        current = (scale_column * total).astype(jnp.bfloat16)
        if hop < HOPS - 1:
            following = (scale_column * current.astype(jnp.float32)).astype(jnp.bfloat16)
            following = following.reshape(PAIR, n_rep, rows, group_width)
            for c in range(PAIR):
                gathered[hop + 1, :, chip * PAIR + c] = following[c]
            hop_copies.append(send_hop(hop + 1))
        hops[hop] = current.reshape(PAIR, n_rep, rows, group_width)
        mine = pl.ds(pl.multiple_of(group * group_width, LANES), group_width)
        for step in range(1, groups):
            other, device = column_peer(step)
            copy = remote(hops.at[hop, lax.rem(other, PAIR), other // PAIR],
                          outs[hop].at[:, mine],
                          out_send.at[hop, step - 1], out_recv.at[hop, step - 1], device)
            copy.start()
            out_copies.append(copy)
        outs[hop][:, mine] = hops[hop, core, rep]

    for copy in out_copies:
        copy.wait_recv()
    for copies in [feature_copies, scale_copies, adjacency_copies, pass_copies, out_copies] + hop_copies:
        for copy in copies:
            copy.wait_send()


def exchange_columns(n_team, n_rep, features, degree, blocks, block_cols, block_count):
    rows, width = features.shape
    groups = n_rep * PAIR
    chips = n_team // PAIR
    group_width = width // groups
    panel = n_rep * rows
    dma = pltpu.SemaphoreType.DMA
    vmem = pl.BlockSpec(memory_space=pltpu.VMEM)
    smem = pl.BlockSpec(memory_space=pltpu.SMEM)
    result = jax.ShapeDtypeStruct((rows, width), jnp.bfloat16)
    return pl.pallas_call(
        functools.partial(diffuse_kernel, n_team, n_rep),
        out_shape=(result,) * HOPS,
        in_specs=[vmem, vmem, vmem, smem, smem],
        out_specs=(vmem,) * HOPS,
        scratch_shapes=[
            pltpu.VMEM((groups, rows, group_width), jnp.bfloat16),
            pltpu.VMEM((HOPS, n_rep, n_team, rows, group_width), jnp.bfloat16),
            pltpu.VMEM((n_rep, PAIR, panel, n_team * rows), jnp.bfloat16),
            pltpu.VMEM((PAIR, n_rep, 8, LANES), jnp.float32),
            pltpu.VMEM((HOPS, PAIR, n_rep, rows, group_width), jnp.bfloat16),
            dma((groups - 1,)), dma((groups - 1,)),
            dma((groups - 1,)), dma((groups - 1,)),
            dma((n_rep - 1,)), dma((n_rep - 1,)),
            dma((n_rep,)), dma((n_rep,)),
            dma((HOPS, chips - 1)), dma((HOPS, chips - 1)),
            dma((HOPS, groups - 1)), dma((HOPS, groups - 1)),
        ],
        compiler_params=pltpu.CompilerParams(
            collective_id=0, has_side_effects=True, vmem_limit_bytes=24 * 1024 * 1024),
    )(features, degree[None, :], blocks, block_cols, block_count)


def gather_and_scatter(features, degree, blocks, block_cols, block_count):
    width = features.shape[1]
    block_size = blocks.shape[-1]
    row_blocks = blocks.shape[0]
    col_blocks = blocks.shape[2]
    panel = row_blocks * block_size
    tiles = blocks[:, 0]
    columns_used = block_cols[:, 0]
    counts_used = block_count[:, 0]
    scale = lax.rsqrt(degree.astype(jnp.float32))[:, None]
    current = features
    results = []
    for hop in range(HOPS):
        sent = (scale * current.astype(jnp.float32)).astype(jnp.bfloat16)
        whole = lax.all_gather(sent, "team", axis=0, tiled=True)
        pieces = whole.reshape(col_blocks, block_size, width)

        def row_block(which, accum):

            def add_slot(slot, inner):
                tile = tiles[which, slot]
                piece = pieces[columns_used[which, slot]]
                return inner + jnp.dot(tile, piece, preferred_element_type=jnp.float32)

            block_rows = lax.fori_loop(
                0, counts_used[which], add_slot, jnp.zeros((block_size, width), jnp.float32)
            )
            return lax.dynamic_update_slice_in_dim(accum, block_rows, which * block_size, 0)

        partial_value = lax.fori_loop(
            0, row_blocks, row_block, jnp.zeros((panel, width), jnp.float32)
        )
        total = lax.psum_scatter(
            partial_value.astype(jnp.bfloat16), "rep", scatter_dimension=0, tiled=True
        ).astype(jnp.float32)
        current = (scale * (total + sent.astype(jnp.float32))).astype(jnp.bfloat16)
        results.append(current)
    return (results[0], results[1], results[2])


def fits_columns(n_team, n_rep, features, blocks):
    rows, width = features.shape
    return (width % (n_rep * PAIR * LANES) == 0 and n_team % PAIR == 0 and n_team > PAIR
            and n_rep > 1 and blocks.shape[0] == 1 and rows % 16 == 0 and rows <= LANES
            and blocks.shape[-1] == n_rep * rows
            and blocks.shape[-1] % LANES == 0
            and n_rep * n_team * rows * n_rep * rows * 4 <= 4 * 1024 * 1024)


def solution(mesh):
    n_team, n_rep = mesh.shape["team"], mesh.shape["rep"]

    def on_device(features, degree, blocks, block_cols, block_count):
        arrays = (features, degree, blocks, block_cols, block_count)
        if fits_columns(n_team, n_rep, features, blocks):
            return exchange_columns(n_team, n_rep, *arrays)
        return gather_and_scatter(*arrays)

    in_specs = (
        P(("team", "rep"), None),
        P(("team", "rep")),
        P("team", "rep", None, None, None),
        P("team", "rep", None),
        P("team", "rep"),
    )
    out_specs = (P(("team", "rep"), None), P(("team", "rep"), None), P(("team", "rep"), None))
    return jax.shard_map(
        on_device, mesh=mesh, in_specs=in_specs, out_specs=out_specs, check_vma=False
    )
```

```python
import functools

import jax
import jax.numpy as jnp
from jax import lax
from jax.experimental import pallas as pl
from jax.experimental.pallas import tpu as pltpu
from jax.sharding import PartitionSpec as P

HOPS = 3
PAIR = 2
LANES = 128
MESH_IDS = pl.DeviceIdType.MESH


def diffuse_kernel(n_team, n_rep, features_in, degree_in, blocks_in, cols_in, count_in,
                   out1, out2, out3, features, degree, blocks, block_cols, block_count,
                   sent, gathered, adjacency, scales, hops, in_sem,
                   feat_send, feat_recv, scale_send, scale_recv, adj_send, adj_recv,
                   pass_send, pass_recv, hop_send, hop_recv, out_send, out_recv, keep_sem):
    groups = n_rep * PAIR
    chips = n_team // PAIR
    rows, width = features.shape
    group_width = width // groups
    slots, block_size = blocks.shape[2], blocks.shape[-1]
    panel = n_rep * rows
    col_blocks = n_team * rows // block_size
    team_run = n_team // col_blocks
    team, rep = lax.axis_index("team"), lax.axis_index("rep")
    chip, core = team // PAIR, lax.rem(team, PAIR)
    group = rep * PAIR + core
    outs = (out1, out2, out3)

    loads = []
    for index, (src, dst) in enumerate(((features_in, features), (degree_in, degree),
                                        (blocks_in, blocks), (cols_in, block_cols),
                                        (count_in, block_count))):
        copy = pltpu.make_async_copy(src, dst, in_sem.at[index])
        copy.start()
        loads.append(copy)

    def column_peer(step):
        other = lax.rem(group + step, groups)
        return other, (chip * PAIR + lax.rem(other, PAIR), other // PAIR)

    def plane_peer(step):
        other = (chip + 1 - 2 * lax.rem(chip, 2), lax.rem(chip + 2, chips), chips - 1 - chip)[step - 1]
        return (other * PAIR + core, rep)

    def remote(src, dst, send_sem, recv_sem, device):
        return pltpu.make_async_remote_copy(
            src_ref=src, dst_ref=dst, send_sem=send_sem, recv_sem=recv_sem,
            device_id=device, device_id_type=MESH_IDS)

    barrier = pltpu.get_barrier_semaphore()
    for step in range(1, groups):
        pl.semaphore_signal(barrier, inc=1, device_id=column_peer(step)[1], device_id_type=MESH_IDS)
    for step in range(1, chips):
        pl.semaphore_signal(barrier, inc=1, device_id=plane_peer(step), device_id_type=MESH_IDS)

    for copy in loads:
        copy.wait()
    own_scale = lax.rsqrt(degree[...].astype(jnp.float32))

    def as_column(row):
        on_diagonal = (lax.broadcasted_iota(jnp.int32, (rows, rows), 0)
                       == lax.broadcasted_iota(jnp.int32, (rows, rows), 1))
        spread = jnp.where(on_diagonal, jnp.broadcast_to(row, (rows, rows)), 0.0)
        return jnp.sum(spread, axis=1, keepdims=True)

    own_column = as_column(own_scale)
    for index in range(groups):
        part = features[:, index * group_width:(index + 1) * group_width].astype(jnp.float32)
        sent[index] = (own_column * part).astype(jnp.bfloat16)
    scales[core, rep, 0:1, 0:rows] = own_scale

    def replica_columns(which):
        return pl.ds(pl.multiple_of(which * block_size, LANES), block_size)

    for column in range(col_blocks):
        dense = jnp.zeros((block_size, block_size), jnp.float32)
        for slot in range(slots):
            used = (block_cols[0, 0, slot] == column) & (slot < block_count[0, 0])
            factor = jnp.where(used, 1.0, 0.0).astype(jnp.float32)
            dense = dense + factor * blocks[0, 0, slot].astype(jnp.float32)
        adjacency[column, core, :, replica_columns(rep)] = dense.astype(jnp.bfloat16)

    pl.semaphore_wait(barrier, groups - 1 + chips - 1)

    feature_copies, scale_copies, adjacency_copies, pass_copies = [], [], [], []
    for step in range(1, groups):
        other, device = column_peer(step)
        copy = remote(sent.at[other], gathered.at[0, rep, team],
                      feat_send.at[step - 1], feat_recv.at[step - 1], device)
        copy.start()
        feature_copies.append(copy)

    def adjacency_of(which):
        return adjacency.at[:, core, :, replica_columns(which)]

    sibling = (chip * PAIR + lax.rem(core + 1, PAIR), rep)
    for step in range(1, n_rep):
        copy = remote(adjacency_of(rep), adjacency_of(rep),
                      adj_send.at[step - 1], adj_recv.at[step - 1],
                      (team, lax.rem(rep + step, n_rep)))
        copy.start()
        adjacency_copies.append(copy)
    copy = remote(adjacency_of(rep), adjacency_of(rep), pass_send.at[0], pass_recv.at[0], sibling)
    copy.start()
    pass_copies.append(copy)
    for step in range(1, groups):
        copy = remote(scales.at[core, rep], scales.at[core, rep],
                      scale_send.at[step - 1], scale_recv.at[step - 1], column_peer(step)[1])
        copy.start()
        scale_copies.append(copy)
    gathered[0, rep, team] = sent[group]

    panels = (lax.rem(core + 1, PAIR), core)

    def send_hop(hop, half):
        copies = []
        own = gathered.at[hop, :, chip * PAIR + panels[half]]
        for step in (1, 3, 2):
            copy = remote(own, own, hop_send.at[hop, half, step - 1],
                          hop_recv.at[hop, half, step - 1], plane_peer(step))
            copy.start()
            copies.append(copy)
        return copies

    for copy in feature_copies:
        copy.wait_recv()
    hop_copies = [[send_hop(0, half) for half in range(PAIR)]]

    for step in range(1, n_rep):
        adjacency_copies[step - 1].wait_recv()
        source = lax.rem(rep + n_rep - step, n_rep)
        copy = remote(adjacency_of(source), adjacency_of(source),
                      pass_send.at[step], pass_recv.at[step], sibling)
        copy.start()
        pass_copies.append(copy)
    for copy in scale_copies:
        copy.wait_recv()
    scale_columns = [
        jnp.concatenate([as_column(scales[c, r, 0:1, 0:rows]) for r in range(n_rep)], axis=0)
        for c in panels]
    for copy in pass_copies:
        copy.wait_recv()

    near = team // team_run
    mine = pl.ds(pl.multiple_of(group * group_width, LANES), group_width)

    def product(hop, column, c):
        piece = gathered[hop, :, pl.ds(column * team_run, team_run)]
        return jnp.dot(adjacency[column, c], piece.reshape(n_rep * block_size, group_width),
                       preferred_element_type=jnp.float32)

    out_copies, kept_copies = [], []
    for hop in range(HOPS):
        for copies in hop_copies[hop]:
            copies[0].wait_recv()
        totals = []
        for c in panels:
            own = gathered[hop, :, chip * PAIR + c].reshape(panel, group_width)
            totals.append(own.astype(jnp.float32) + product(hop, near, c))
        for copies in hop_copies[hop]:
            for copy in copies[1:]:
                copy.wait_recv()
        if hop < HOPS - 1:
            hop_copies.append([])
        for half, c in enumerate(panels):
            total = totals[half] + product(hop, col_blocks - 1 - near, c)
            current = (scale_columns[half] * total).astype(jnp.bfloat16)
            if hop < HOPS - 1:
                following = (scale_columns[half] * current.astype(jnp.float32)).astype(jnp.bfloat16)
                gathered[hop + 1, :, chip * PAIR + c] = following.reshape(n_rep, rows, group_width)
                hop_copies[hop + 1].append(send_hop(hop + 1, half))
            hops[hop, c] = current.reshape(n_rep, rows, group_width)
            for step in range(1, groups):
                if step % PAIR == 1 - half:
                    other, device = column_peer(step)
                    copy = remote(hops.at[hop, c, other // PAIR], outs[hop].at[:, mine],
                                  out_send.at[hop, step - 1], out_recv.at[hop, step - 1], device)
                    copy.start()
                    out_copies.append(copy)
        kept = pltpu.make_async_copy(hops.at[hop, core, rep], outs[hop].at[:, mine], keep_sem.at[hop])
        kept.start()
        kept_copies.append(kept)

    for copy in out_copies:
        copy.wait_recv()
    for copy in kept_copies:
        copy.wait()
    for copies in [feature_copies, scale_copies, adjacency_copies, pass_copies, out_copies]:
        for copy in copies:
            copy.wait_send()
    for halves in hop_copies:
        for copies in halves:
            for copy in copies:
                copy.wait_send()


def store_kernel(in1, in2, in3, out1, out2, out3, sem):
    copies = [pltpu.make_async_copy(src, dst, sem.at[index])
              for index, (src, dst) in enumerate(((in1, out1), (in2, out2), (in3, out3)))]
    for copy in copies:
        copy.start()
    for copy in copies:
        copy.wait()


def exchange_columns(n_team, n_rep, features, degree, blocks, block_cols, block_count):
    rows, width = features.shape
    groups = n_rep * PAIR
    chips = n_team // PAIR
    group_width = width // groups
    panel = n_rep * rows
    col_blocks = n_team * rows // panel
    dma = pltpu.SemaphoreType.DMA
    hbm = pl.BlockSpec(memory_space=pltpu.HBM)
    result = jax.ShapeDtypeStruct((rows, width), jnp.bfloat16)
    results = pl.pallas_call(
        functools.partial(diffuse_kernel, n_team, n_rep),
        out_shape=(result,) * HOPS,
        in_specs=[hbm] * 5,
        out_specs=(hbm,) * HOPS,
        scratch_shapes=[
            pltpu.VMEM((rows, width), jnp.bfloat16),
            pltpu.VMEM((1, rows), jnp.int32),
            pltpu.VMEM(blocks.shape, jnp.bfloat16),
            pltpu.SMEM(block_cols.shape, jnp.int32),
            pltpu.SMEM(block_count.shape, jnp.int32),
            pltpu.VMEM((groups, rows, group_width), jnp.bfloat16),
            pltpu.VMEM((HOPS, n_rep, n_team, rows, group_width), jnp.bfloat16),
            pltpu.VMEM((col_blocks, PAIR, panel, n_rep * panel), jnp.bfloat16),
            pltpu.VMEM((PAIR, n_rep, 8, LANES), jnp.float32),
            pltpu.VMEM((HOPS, PAIR, n_rep, rows, group_width), jnp.bfloat16),
            dma((5,)),
            dma((groups - 1,)), dma((groups - 1,)),
            dma((groups - 1,)), dma((groups - 1,)),
            dma((n_rep - 1,)), dma((n_rep - 1,)),
            dma((n_rep,)), dma((n_rep,)),
            dma((HOPS, PAIR, chips - 1)), dma((HOPS, PAIR, chips - 1)),
            dma((HOPS, groups - 1)), dma((HOPS, groups - 1)),
            dma((HOPS,)),
        ],
        compiler_params=pltpu.CompilerParams(
            collective_id=0, has_side_effects=True, vmem_limit_bytes=62 * 1024 * 1024),
    )(features, degree[None, :], blocks, block_cols, block_count)
    return pl.pallas_call(
        store_kernel,
        out_shape=(result,) * HOPS,
        in_specs=[hbm] * HOPS,
        out_specs=(hbm,) * HOPS,
        scratch_shapes=[dma((HOPS,))],
        compiler_params=pltpu.CompilerParams(vmem_limit_bytes=62 * 1024 * 1024),
    )(*results)


def gather_and_scatter(features, degree, blocks, block_cols, block_count):
    width = features.shape[1]
    block_size = blocks.shape[-1]
    row_blocks = blocks.shape[0]
    col_blocks = blocks.shape[2]
    panel = row_blocks * block_size
    tiles = blocks[:, 0]
    columns_used = block_cols[:, 0]
    counts_used = block_count[:, 0]
    scale = lax.rsqrt(degree.astype(jnp.float32))[:, None]
    current = features
    results = []
    for hop in range(HOPS):
        sent = (scale * current.astype(jnp.float32)).astype(jnp.bfloat16)
        whole = lax.all_gather(sent, "team", axis=0, tiled=True)
        pieces = whole.reshape(col_blocks, block_size, width)

        def row_block(which, accum):

            def add_slot(slot, inner):
                tile = tiles[which, slot]
                piece = pieces[columns_used[which, slot]]
                return inner + jnp.dot(tile, piece, preferred_element_type=jnp.float32)

            block_rows = lax.fori_loop(
                0, counts_used[which], add_slot, jnp.zeros((block_size, width), jnp.float32)
            )
            return lax.dynamic_update_slice_in_dim(accum, block_rows, which * block_size, 0)

        partial_value = lax.fori_loop(
            0, row_blocks, row_block, jnp.zeros((panel, width), jnp.float32)
        )
        total = lax.psum_scatter(
            partial_value.astype(jnp.bfloat16), "rep", scatter_dimension=0, tiled=True
        ).astype(jnp.float32)
        current = (scale * (total + sent.astype(jnp.float32))).astype(jnp.bfloat16)
        results.append(current)
    return (results[0], results[1], results[2])


def fits_columns(n_team, n_rep, features, blocks):
    rows, width = features.shape
    return (width % (n_rep * PAIR * LANES) == 0 and n_team == 4 * PAIR
            and n_team * rows == 2 * blocks.shape[-1]
            and n_rep > 1 and blocks.shape[0] == 1 and rows % 16 == 0 and rows <= LANES
            and blocks.shape[-1] == n_rep * rows
            and blocks.shape[-1] % LANES == 0
            and n_rep * n_team * rows * n_rep * rows * 4 <= 4 * 1024 * 1024)


def solution(mesh):
    n_team, n_rep = mesh.shape["team"], mesh.shape["rep"]

    def on_device(features, degree, blocks, block_cols, block_count):
        arrays = (features, degree, blocks, block_cols, block_count)
        if fits_columns(n_team, n_rep, features, blocks):
            return exchange_columns(n_team, n_rep, *arrays)
        return gather_and_scatter(*arrays)

    in_specs = (
        P(("team", "rep"), None),
        P(("team", "rep")),
        P("team", "rep", None, None, None),
        P("team", "rep", None),
        P("team", "rep"),
    )
    out_specs = (P(("team", "rep"), None), P(("team", "rep"), None), P(("team", "rep"), None))
    return jax.shard_map(
        on_device, mesh=mesh, in_specs=in_specs, out_specs=out_specs, check_vma=False
    )
```

```python
import functools

import jax
import jax.numpy as jnp
from jax import lax
from jax.experimental import pallas as pl
from jax.experimental.pallas import tpu as pltpu
from jax.sharding import PartitionSpec as P

HOPS = 3
PAIR = 2
LANES = 128
MESH_IDS = pl.DeviceIdType.MESH


def diffuse_kernel(n_team, n_rep, features_in, degree_in, blocks_in, cols_in, count_in,
                   out1, out2, out3, features, degree, blocks, block_cols, block_count,
                   sent, gathered, adjacency, scales, hops, in_sem,
                   feat_send, feat_recv, scale_send, scale_recv, adj_send, adj_recv,
                   pass_send, pass_recv, hop_send, hop_recv, out_send, out_recv, keep_sem):
    groups = n_rep * PAIR
    chips = n_team // PAIR
    rows, width = features.shape
    group_width = width // groups
    slots, block_size = blocks.shape[2], blocks.shape[-1]
    panel = n_rep * rows
    col_blocks = n_team * rows // block_size
    team_run = n_team // col_blocks
    team, rep = lax.axis_index("team"), lax.axis_index("rep")
    chip, core = team // PAIR, lax.rem(team, PAIR)
    group = rep * PAIR + core
    outs = (out1, out2, out3)

    loads = []
    for index, (src, dst) in enumerate(((features_in, features), (degree_in, degree),
                                        (blocks_in, blocks), (cols_in, block_cols),
                                        (count_in, block_count))):
        copy = pltpu.make_async_copy(src, dst, in_sem.at[index])
        copy.start()
        loads.append(copy)

    def column_peer(step):
        other = lax.rem(group + step, groups)
        return other, (chip * PAIR + lax.rem(other, PAIR), other // PAIR)

    def plane_peer(step):
        other = (chip + 1 - 2 * lax.rem(chip, 2), lax.rem(chip + 2, chips), chips - 1 - chip)[step - 1]
        return (other * PAIR + core, rep)

    def remote(src, dst, send_sem, recv_sem, device):
        return pltpu.make_async_remote_copy(
            src_ref=src, dst_ref=dst, send_sem=send_sem, recv_sem=recv_sem,
            device_id=device, device_id_type=MESH_IDS)

    barrier = pltpu.get_barrier_semaphore()
    for step in range(1, groups):
        pl.semaphore_signal(barrier, inc=1, device_id=column_peer(step)[1], device_id_type=MESH_IDS)
    for step in range(1, chips):
        pl.semaphore_signal(barrier, inc=1, device_id=plane_peer(step), device_id_type=MESH_IDS)

    for copy in loads:
        copy.wait()
    own_scale = lax.rsqrt(degree[...].astype(jnp.float32))

    def as_column(row):
        on_diagonal = (lax.broadcasted_iota(jnp.int32, (rows, rows), 0)
                       == lax.broadcasted_iota(jnp.int32, (rows, rows), 1))
        spread = jnp.where(on_diagonal, jnp.broadcast_to(row, (rows, rows)), 0.0)
        return jnp.sum(spread, axis=1, keepdims=True)

    own_column = as_column(own_scale)
    for index in range(groups):
        part = features[:, index * group_width:(index + 1) * group_width].astype(jnp.float32)
        sent[index] = (own_column * part).astype(jnp.bfloat16)
    scales[core, rep, 0:1, 0:rows] = own_scale

    for column in range(col_blocks):
        dense = jnp.zeros((block_size, block_size), jnp.float32)
        for slot in range(slots):
            used = (block_cols[0, 0, slot] == column) & (slot < block_count[0, 0])
            factor = jnp.where(used, 1.0, 0.0).astype(jnp.float32)
            dense = dense + factor * blocks[0, 0, slot].astype(jnp.float32)
        adjacency[rep, core, column] = dense.astype(jnp.bfloat16)

    pl.semaphore_wait(barrier, groups - 1 + chips - 1)

    feature_copies, scale_copies, adjacency_copies, pass_copies = [], [], [], []
    for step in range(1, groups):
        other, device = column_peer(step)
        copy = remote(sent.at[other], gathered.at[0, rep, team],
                      feat_send.at[step - 1], feat_recv.at[step - 1], device)
        copy.start()
        feature_copies.append(copy)

    def adjacency_of(which):
        return adjacency.at[which, core]

    sibling = (chip * PAIR + lax.rem(core + 1, PAIR), rep)
    for step in range(1, n_rep):
        copy = remote(adjacency_of(rep), adjacency_of(rep),
                      adj_send.at[step - 1], adj_recv.at[step - 1],
                      (team, lax.rem(rep + step, n_rep)))
        copy.start()
        adjacency_copies.append(copy)
    copy = remote(adjacency_of(rep), adjacency_of(rep), pass_send.at[0], pass_recv.at[0], sibling)
    copy.start()
    pass_copies.append(copy)
    for step in range(1, groups):
        copy = remote(scales.at[core, rep], scales.at[core, rep],
                      scale_send.at[step - 1], scale_recv.at[step - 1], column_peer(step)[1])
        copy.start()
        scale_copies.append(copy)
    gathered[0, rep, team] = sent[group]

    panels = (lax.rem(core + 1, PAIR), core)

    def send_hop(hop, half):
        copies = []
        own = gathered.at[hop, :, chip * PAIR + panels[half]]
        for step in (1, 3, 2):
            copy = remote(own, own, hop_send.at[hop, half, step - 1],
                          hop_recv.at[hop, half, step - 1], plane_peer(step))
            copy.start()
            copies.append(copy)
        return copies

    for copy in feature_copies:
        copy.wait_recv()
    hop_copies = [[send_hop(0, half) for half in range(PAIR)]]

    for step in range(1, n_rep):
        adjacency_copies[step - 1].wait_recv()
        source = lax.rem(rep + n_rep - step, n_rep)
        copy = remote(adjacency_of(source), adjacency_of(source),
                      pass_send.at[step], pass_recv.at[step], sibling)
        copy.start()
        pass_copies.append(copy)
    for copy in scale_copies:
        copy.wait_recv()
    scale_columns = [
        jnp.concatenate([as_column(scales[c, r, 0:1, 0:rows]) for r in range(n_rep)], axis=0)
        for c in panels]

    near = team // team_run
    mine = pl.ds(pl.multiple_of(group * group_width, LANES), group_width)

    def product(hop, column, c):
        piece = gathered[hop, :, pl.ds(column * team_run, team_run)]
        weights = jnp.concatenate([adjacency[r, c, column] for r in range(n_rep)], axis=1)
        return jnp.dot(weights, piece.reshape(n_rep * block_size, group_width),
                       preferred_element_type=jnp.float32)

    out_copies, kept_copies = [], []
    for hop in range(HOPS):
        for copies in hop_copies[hop]:
            copies[0].wait_recv()
        totals = [gathered[hop, :, chip * PAIR + c].reshape(panel, group_width).astype(jnp.float32)
                  for c in panels]
        if hop == 0:
            for copies in hop_copies[hop]:
                for copy in copies[1:]:
                    copy.wait_recv()
            for step in range(n_rep):
                pass_copies[step].wait_recv()
                source = lax.rem(rep + n_rep - step, n_rep)
                piece = gathered[hop, source].reshape(col_blocks * block_size, group_width)
                for half, c in enumerate(panels):
                    weights = jnp.concatenate(
                        [adjacency[source, c, column] for column in range(col_blocks)], axis=1)
                    totals[half] = totals[half] + jnp.dot(
                        weights, piece, preferred_element_type=jnp.float32)
        else:
            for half, c in enumerate(panels):
                totals[half] = totals[half] + product(hop, near, c)
            for copies in hop_copies[hop]:
                for copy in copies[1:]:
                    copy.wait_recv()
        if hop < HOPS - 1:
            hop_copies.append([])
        for half, c in enumerate(panels):
            total = totals[half]
            if hop > 0:
                total = total + product(hop, col_blocks - 1 - near, c)
            current = (scale_columns[half] * total).astype(jnp.bfloat16)
            if hop < HOPS - 1:
                following = (scale_columns[half] * current.astype(jnp.float32)).astype(jnp.bfloat16)
                gathered[hop + 1, :, chip * PAIR + c] = following.reshape(n_rep, rows, group_width)
                hop_copies[hop + 1].append(send_hop(hop + 1, half))
            hops[hop, c] = current.reshape(n_rep, rows, group_width)
            for step in range(1, groups):
                if step % PAIR == 1 - half:
                    other, device = column_peer(step)
                    copy = remote(hops.at[hop, c, other // PAIR], outs[hop].at[:, mine],
                                  out_send.at[hop, step - 1], out_recv.at[hop, step - 1], device)
                    copy.start()
                    out_copies.append(copy)
        kept = pltpu.make_async_copy(hops.at[hop, core, rep], outs[hop].at[:, mine], keep_sem.at[hop])
        kept.start()
        kept_copies.append(kept)

    for copy in out_copies:
        copy.wait_recv()
    for copy in kept_copies:
        copy.wait()
    for copies in [feature_copies, scale_copies, adjacency_copies, pass_copies, out_copies]:
        for copy in copies:
            copy.wait_send()
    for halves in hop_copies:
        for copies in halves:
            for copy in copies:
                copy.wait_send()


def store_kernel(in1, in2, in3, out1, out2, out3, held, load_sem, store_sem):
    refs = ((in1, out1), (in2, out2), (in3, out3))
    loads = [pltpu.make_async_copy(src, held.at[index], load_sem.at[index])
             for index, (src, dst) in enumerate(refs)]
    stores = [pltpu.make_async_copy(held.at[index], dst, store_sem.at[index])
              for index, (src, dst) in enumerate(refs)]
    for load in loads:
        load.start()
    for load, store in zip(loads, stores):
        load.wait()
        store.start()
    for store in stores:
        store.wait()


def exchange_columns(n_team, n_rep, features, degree, blocks, block_cols, block_count):
    rows, width = features.shape
    groups = n_rep * PAIR
    chips = n_team // PAIR
    group_width = width // groups
    panel = n_rep * rows
    col_blocks = n_team * rows // panel
    dma = pltpu.SemaphoreType.DMA
    hbm = pl.BlockSpec(memory_space=pltpu.HBM)
    result = jax.ShapeDtypeStruct((rows, width), jnp.bfloat16)
    results = pl.pallas_call(
        functools.partial(diffuse_kernel, n_team, n_rep),
        out_shape=(result,) * HOPS,
        in_specs=[hbm] * 5,
        out_specs=(hbm,) * HOPS,
        scratch_shapes=[
            pltpu.VMEM((rows, width), jnp.bfloat16),
            pltpu.VMEM((1, rows), jnp.int32),
            pltpu.VMEM(blocks.shape, jnp.bfloat16),
            pltpu.SMEM(block_cols.shape, jnp.int32),
            pltpu.SMEM(block_count.shape, jnp.int32),
            pltpu.VMEM((groups, rows, group_width), jnp.bfloat16),
            pltpu.VMEM((HOPS, n_rep, n_team, rows, group_width), jnp.bfloat16),
            pltpu.VMEM((n_rep, PAIR, col_blocks, panel, panel), jnp.bfloat16),
            pltpu.VMEM((PAIR, n_rep, 8, LANES), jnp.float32),
            pltpu.VMEM((HOPS, PAIR, n_rep, rows, group_width), jnp.bfloat16),
            dma((5,)),
            dma((groups - 1,)), dma((groups - 1,)),
            dma((groups - 1,)), dma((groups - 1,)),
            dma((n_rep - 1,)), dma((n_rep - 1,)),
            dma((n_rep,)), dma((n_rep,)),
            dma((HOPS, PAIR, chips - 1)), dma((HOPS, PAIR, chips - 1)),
            dma((HOPS, groups - 1)), dma((HOPS, groups - 1)),
            dma((HOPS,)),
        ],
        compiler_params=pltpu.CompilerParams(
            collective_id=0, has_side_effects=True, vmem_limit_bytes=62 * 1024 * 1024),
    )(features, degree[None, :], blocks, block_cols, block_count)
    return pl.pallas_call(
        store_kernel,
        out_shape=(result,) * HOPS,
        in_specs=[hbm] * HOPS,
        out_specs=(hbm,) * HOPS,
        scratch_shapes=[pltpu.VMEM((HOPS, rows, width), jnp.bfloat16), dma((HOPS,)), dma((HOPS,))],
        compiler_params=pltpu.CompilerParams(vmem_limit_bytes=62 * 1024 * 1024),
    )(*results)


def gather_and_scatter(features, degree, blocks, block_cols, block_count):
    width = features.shape[1]
    block_size = blocks.shape[-1]
    row_blocks = blocks.shape[0]
    col_blocks = blocks.shape[2]
    panel = row_blocks * block_size
    tiles = blocks[:, 0]
    columns_used = block_cols[:, 0]
    counts_used = block_count[:, 0]
    scale = lax.rsqrt(degree.astype(jnp.float32))[:, None]
    current = features
    results = []
    for hop in range(HOPS):
        sent = (scale * current.astype(jnp.float32)).astype(jnp.bfloat16)
        whole = lax.all_gather(sent, "team", axis=0, tiled=True)
        pieces = whole.reshape(col_blocks, block_size, width)

        def row_block(which, accum):

            def add_slot(slot, inner):
                tile = tiles[which, slot]
                piece = pieces[columns_used[which, slot]]
                return inner + jnp.dot(tile, piece, preferred_element_type=jnp.float32)

            block_rows = lax.fori_loop(
                0, counts_used[which], add_slot, jnp.zeros((block_size, width), jnp.float32)
            )
            return lax.dynamic_update_slice_in_dim(accum, block_rows, which * block_size, 0)

        partial_value = lax.fori_loop(
            0, row_blocks, row_block, jnp.zeros((panel, width), jnp.float32)
        )
        total = lax.psum_scatter(
            partial_value.astype(jnp.bfloat16), "rep", scatter_dimension=0, tiled=True
        ).astype(jnp.float32)
        current = (scale * (total + sent.astype(jnp.float32))).astype(jnp.bfloat16)
        results.append(current)
    return (results[0], results[1], results[2])


def fits_columns(n_team, n_rep, features, blocks):
    rows, width = features.shape
    return (width % (n_rep * PAIR * LANES) == 0 and n_team == 4 * PAIR
            and n_team * rows == 2 * blocks.shape[-1]
            and n_rep > 1 and blocks.shape[0] == 1 and rows % 16 == 0 and rows <= LANES
            and blocks.shape[-1] == n_rep * rows
            and blocks.shape[-1] % LANES == 0
            and n_rep * n_team * rows * n_rep * rows * 4 <= 4 * 1024 * 1024)


def solution(mesh):
    n_team, n_rep = mesh.shape["team"], mesh.shape["rep"]

    def on_device(features, degree, blocks, block_cols, block_count):
        arrays = (features, degree, blocks, block_cols, block_count)
        if fits_columns(n_team, n_rep, features, blocks):
            return exchange_columns(n_team, n_rep, *arrays)
        return gather_and_scatter(*arrays)

    in_specs = (
        P(("team", "rep"), None),
        P(("team", "rep")),
        P("team", "rep", None, None, None),
        P("team", "rep", None),
        P("team", "rep"),
    )
    out_specs = (P(("team", "rep"), None), P(("team", "rep"), None), P(("team", "rep"), None))
    return jax.shard_map(
        on_device, mesh=mesh, in_specs=in_specs, out_specs=out_specs, check_vma=False
    )
```

```python
import functools

import jax
import jax.numpy as jnp
from jax import lax
from jax.experimental import pallas as pl
from jax.experimental.pallas import tpu as pltpu
from jax.sharding import PartitionSpec as P

HOPS = 3
PAIR = 2
LANES = 128
MESH_IDS = pl.DeviceIdType.MESH


def diffuse_kernel(n_team, n_rep, features_in, degree_in, blocks_in, cols_in, count_in,
                   out, features, degree, blocks, block_cols, block_count,
                   sent, arrived, gathered, adjacency, hops, in_sem,
                   feat_send, feat_recv, adj_send, adj_recv,
                   pass_send, pass_recv, hop_send, hop_recv, out_send, out_recv, keep_sem):
    groups = n_rep * PAIR
    chips = n_team // PAIR
    rows, width = features.shape
    group_width = width // groups
    slots, block_size = blocks.shape[2], blocks.shape[-1]
    panel = n_rep * rows
    col_blocks = n_team * rows // block_size
    team_run = n_team // col_blocks
    team, rep = lax.axis_index("team"), lax.axis_index("rep")
    chip, core = team // PAIR, lax.rem(team, PAIR)
    group = rep * PAIR + core

    loads = []
    for index, (src, dst) in enumerate(((features_in, features), (degree_in, degree),
                                        (blocks_in, blocks), (cols_in, block_cols),
                                        (count_in, block_count))):
        copy = pltpu.make_async_copy(src, dst, in_sem.at[index])
        copy.start()
        loads.append(copy)

    def column_peer(step):
        other = lax.rem(group + step, groups)
        return other, (chip * PAIR + lax.rem(other, PAIR), other // PAIR)

    def plane_peer(step):
        other = (chip + 1 - 2 * lax.rem(chip, 2), lax.rem(chip + 2, chips), chips - 1 - chip)[step - 1]
        return (other * PAIR + core, rep)

    def remote(src, dst, send_sem, recv_sem, device):
        return pltpu.make_async_remote_copy(
            src_ref=src, dst_ref=dst, send_sem=send_sem, recv_sem=recv_sem,
            device_id=device, device_id_type=MESH_IDS)

    barrier = pltpu.get_barrier_semaphore()
    for step in range(1, groups):
        pl.semaphore_signal(barrier, inc=1, device_id=column_peer(step)[1], device_id_type=MESH_IDS)
    for step in range(1, chips):
        pl.semaphore_signal(barrier, inc=1, device_id=plane_peer(step), device_id_type=MESH_IDS)

    for copy in loads:
        copy.wait()
    own_degree = degree[...].astype(jnp.float32)

    def as_column(row):
        on_diagonal = (lax.broadcasted_iota(jnp.int32, (rows, rows), 0)
                       == lax.broadcasted_iota(jnp.int32, (rows, rows), 1))
        spread = jnp.where(on_diagonal, jnp.broadcast_to(row, (rows, rows)), 0.0)
        return jnp.sum(spread, axis=1, keepdims=True)

    own_column = lax.rsqrt(as_column(own_degree))
    degree_rows = jnp.broadcast_to(jnp.concatenate(
        [own_degree, jnp.ones((1, group_width - rows), jnp.float32)], axis=1), (16, group_width))
    degree_rows = degree_rows.astype(jnp.bfloat16)
    for index in range(groups):
        part = features[:, index * group_width:(index + 1) * group_width].astype(jnp.float32)
        sent[index, 0:rows] = (own_column * part).astype(jnp.bfloat16)
        sent[index, rows:rows + 16] = degree_rows

    for column in range(col_blocks):
        dense = jnp.zeros((block_size, block_size), jnp.float32)
        for slot in range(slots):
            used = (block_cols[0, 0, slot] == column) & (slot < block_count[0, 0])
            factor = jnp.where(used, 1.0, 0.0).astype(jnp.float32)
            dense = dense + factor * blocks[0, 0, slot].astype(jnp.float32)
        adjacency[rep, core, column] = dense.astype(jnp.bfloat16)

    pl.semaphore_wait(barrier, groups - 1 + chips - 1)

    feature_copies, adjacency_copies, pass_copies = [], [], []
    for step in range(1, groups):
        other, device = column_peer(step)
        copy = remote(sent.at[other], arrived.at[rep, core],
                      feat_send.at[step - 1], feat_recv.at[step - 1], device)
        copy.start()
        feature_copies.append(copy)

    def adjacency_of(which):
        return adjacency.at[which, core]

    sibling = (chip * PAIR + lax.rem(core + 1, PAIR), rep)
    for step in range(1, n_rep):
        copy = remote(adjacency_of(rep), adjacency_of(rep),
                      adj_send.at[step - 1], adj_recv.at[step - 1],
                      (team, lax.rem(rep + step, n_rep)))
        copy.start()
        adjacency_copies.append(copy)
    copy = remote(adjacency_of(rep), adjacency_of(rep), pass_send.at[0], pass_recv.at[0], sibling)
    copy.start()
    pass_copies.append(copy)
    arrived[rep, core] = sent[group]

    panels = (lax.rem(core + 1, PAIR), core)

    def send_hop(hop, half):
        copies = []
        own = gathered.at[hop, :, chip * PAIR + panels[half]]
        for step in (1, 3, 2):
            copy = remote(own, own, hop_send.at[hop, half, step - 1],
                          hop_recv.at[hop, half, step - 1], plane_peer(step))
            copy.start()
            copies.append(copy)
        return copies

    for copy in feature_copies:
        copy.wait_recv()
    for c in range(PAIR):
        gathered[0, :, chip * PAIR + c] = arrived[:, c, 0:rows]
    hop_copies = [[send_hop(0, half) for half in range(PAIR)]]

    for step in range(1, n_rep):
        adjacency_copies[step - 1].wait_recv()
        source = lax.rem(rep + n_rep - step, n_rep)
        copy = remote(adjacency_of(source), adjacency_of(source),
                      pass_send.at[step], pass_recv.at[step], sibling)
        copy.start()
        pass_copies.append(copy)
    scale_columns = [
        lax.rsqrt(jnp.concatenate(
            [as_column(arrived[r, c, rows:rows + 16].astype(jnp.float32)[0:1, 0:rows])
             for r in range(n_rep)], axis=0))
        for c in panels]

    near = team // team_run
    mine = pl.ds(pl.multiple_of(group * group_width, LANES), group_width)

    def product(hop, column, c):
        piece = gathered[hop, :, pl.ds(column * team_run, team_run)]
        weights = jnp.concatenate([adjacency[r, c, column] for r in range(n_rep)], axis=1)
        return jnp.dot(weights, piece.reshape(n_rep * block_size, group_width),
                       preferred_element_type=jnp.float32)

    out_copies, kept_copies = [], []
    for hop in range(HOPS):
        for copies in hop_copies[hop]:
            copies[0].wait_recv()
        totals = [gathered[hop, :, chip * PAIR + c].reshape(panel, group_width).astype(jnp.float32)
                  for c in panels]
        if hop == 0:
            for copies in hop_copies[hop]:
                for copy in copies[1:]:
                    copy.wait_recv()
            for step in range(n_rep):
                pass_copies[step].wait_recv()
                source = lax.rem(rep + n_rep - step, n_rep)
                piece = gathered[hop, source].reshape(col_blocks * block_size, group_width)
                for half, c in enumerate(panels):
                    weights = jnp.concatenate(
                        [adjacency[source, c, column] for column in range(col_blocks)], axis=1)
                    totals[half] = totals[half] + jnp.dot(
                        weights, piece, preferred_element_type=jnp.float32)
        else:
            for half, c in enumerate(panels):
                totals[half] = totals[half] + product(hop, near, c)
            for copies in hop_copies[hop]:
                for copy in copies[1:]:
                    copy.wait_recv()
        if hop < HOPS - 1:
            hop_copies.append([])
        for half, c in enumerate(panels):
            total = totals[half]
            if hop > 0:
                total = total + product(hop, col_blocks - 1 - near, c)
            current = (scale_columns[half] * total).astype(jnp.bfloat16)
            if hop < HOPS - 1:
                following = (scale_columns[half] * current.astype(jnp.float32)).astype(jnp.bfloat16)
                gathered[hop + 1, :, chip * PAIR + c] = following.reshape(n_rep, rows, group_width)
                hop_copies[hop + 1].append(send_hop(hop + 1, half))
            hops[hop, c] = current.reshape(n_rep, rows, group_width)
            part = {HOPS - 2: (0, HOPS - 1), HOPS - 1: (HOPS - 1, 1)}.get(hop)
            if part is None:
                continue
            share = pl.ds(*part)
            which = hop - (HOPS - 2)
            for step in range(1, groups):
                if step % PAIR == 1 - half:
                    other, device = column_peer(step)
                    copy = remote(hops.at[share, c, other // PAIR], out.at[share, :, mine],
                                  out_send.at[which, step - 1], out_recv.at[which, step - 1], device)
                    copy.start()
                    out_copies.append(copy)
            if half == PAIR - 1:
                kept = pltpu.make_async_copy(hops.at[share, core, rep], out.at[share, :, mine],
                                             keep_sem.at[which])
                kept.start()
                kept_copies.append(kept)

    for copy in out_copies:
        copy.wait_recv()
    for copy in kept_copies:
        copy.wait()
    for copies in [feature_copies, adjacency_copies, pass_copies, out_copies]:
        for copy in copies:
            copy.wait_send()
    for halves in hop_copies:
        for copies in halves:
            for copy in copies:
                copy.wait_send()


def store_kernel(results, out1, out2, out3, held, load_sem, store_sem):
    refs = tuple((results.at[index], out) for index, out in enumerate((out1, out2, out3)))
    loads = [pltpu.make_async_copy(src, held.at[index], load_sem.at[index])
             for index, (src, dst) in enumerate(refs)]
    stores = [pltpu.make_async_copy(held.at[index], dst, store_sem.at[index])
              for index, (src, dst) in enumerate(refs)]
    for load in loads:
        load.start()
    for load, store in zip(loads, stores):
        load.wait()
        store.start()
    for store in stores:
        store.wait()


def exchange_columns(n_team, n_rep, features, degree, blocks, block_cols, block_count):
    rows, width = features.shape
    groups = n_rep * PAIR
    chips = n_team // PAIR
    group_width = width // groups
    panel = n_rep * rows
    col_blocks = n_team * rows // panel
    dma = pltpu.SemaphoreType.DMA
    hbm = pl.BlockSpec(memory_space=pltpu.HBM)
    result = jax.ShapeDtypeStruct((rows, width), jnp.bfloat16)
    results = pl.pallas_call(
        functools.partial(diffuse_kernel, n_team, n_rep),
        out_shape=jax.ShapeDtypeStruct((HOPS, rows, width), jnp.bfloat16),
        in_specs=[hbm] * 5,
        out_specs=hbm,
        scratch_shapes=[
            pltpu.VMEM((rows, width), jnp.bfloat16),
            pltpu.VMEM((1, rows), jnp.int32),
            pltpu.VMEM(blocks.shape, jnp.bfloat16),
            pltpu.SMEM(block_cols.shape, jnp.int32),
            pltpu.SMEM(block_count.shape, jnp.int32),
            pltpu.VMEM((groups, rows + 16, group_width), jnp.bfloat16),
            pltpu.VMEM((n_rep, PAIR, rows + 16, group_width), jnp.bfloat16),
            pltpu.VMEM((HOPS, n_rep, n_team, rows, group_width), jnp.bfloat16),
            pltpu.VMEM((n_rep, PAIR, col_blocks, panel, panel), jnp.bfloat16),
            pltpu.VMEM((HOPS, PAIR, n_rep, rows, group_width), jnp.bfloat16),
            dma((5,)),
            dma((groups - 1,)), dma((groups - 1,)),
            dma((n_rep - 1,)), dma((n_rep - 1,)),
            dma((n_rep,)), dma((n_rep,)),
            dma((HOPS, PAIR, chips - 1)), dma((HOPS, PAIR, chips - 1)),
            dma((2, groups - 1)), dma((2, groups - 1)),
            dma((2,)),
        ],
        compiler_params=pltpu.CompilerParams(
            collective_id=0, has_side_effects=True, vmem_limit_bytes=62 * 1024 * 1024),
    )(features, degree[None, :], blocks, block_cols, block_count)
    return pl.pallas_call(
        store_kernel,
        out_shape=(result,) * HOPS,
        in_specs=[hbm],
        out_specs=(hbm,) * HOPS,
        scratch_shapes=[pltpu.VMEM((HOPS, rows, width), jnp.bfloat16), dma((HOPS,)), dma((HOPS,))],
        compiler_params=pltpu.CompilerParams(vmem_limit_bytes=62 * 1024 * 1024),
    )(results)


def gather_and_scatter(features, degree, blocks, block_cols, block_count):
    width = features.shape[1]
    block_size = blocks.shape[-1]
    row_blocks = blocks.shape[0]
    col_blocks = blocks.shape[2]
    panel = row_blocks * block_size
    tiles = blocks[:, 0]
    columns_used = block_cols[:, 0]
    counts_used = block_count[:, 0]
    scale = lax.rsqrt(degree.astype(jnp.float32))[:, None]
    current = features
    results = []
    for hop in range(HOPS):
        sent = (scale * current.astype(jnp.float32)).astype(jnp.bfloat16)
        whole = lax.all_gather(sent, "team", axis=0, tiled=True)
        pieces = whole.reshape(col_blocks, block_size, width)

        def row_block(which, accum):

            def add_slot(slot, inner):
                tile = tiles[which, slot]
                piece = pieces[columns_used[which, slot]]
                return inner + jnp.dot(tile, piece, preferred_element_type=jnp.float32)

            block_rows = lax.fori_loop(
                0, counts_used[which], add_slot, jnp.zeros((block_size, width), jnp.float32)
            )
            return lax.dynamic_update_slice_in_dim(accum, block_rows, which * block_size, 0)

        partial_value = lax.fori_loop(
            0, row_blocks, row_block, jnp.zeros((panel, width), jnp.float32)
        )
        total = lax.psum_scatter(
            partial_value.astype(jnp.bfloat16), "rep", scatter_dimension=0, tiled=True
        ).astype(jnp.float32)
        current = (scale * (total + sent.astype(jnp.float32))).astype(jnp.bfloat16)
        results.append(current)
    return (results[0], results[1], results[2])


def fits_columns(n_team, n_rep, features, blocks):
    rows, width = features.shape
    return (width % (n_rep * PAIR * LANES) == 0 and n_team == 4 * PAIR
            and n_team * rows == 2 * blocks.shape[-1]
            and n_rep > 1 and blocks.shape[0] == 1 and rows % 16 == 0 and rows < LANES
            and blocks.shape[-1] == n_rep * rows
            and blocks.shape[-1] % LANES == 0
            and n_rep * n_team * rows * n_rep * rows * 4 <= 4 * 1024 * 1024)


def solution(mesh):
    n_team, n_rep = mesh.shape["team"], mesh.shape["rep"]

    def on_device(features, degree, blocks, block_cols, block_count):
        arrays = (features, degree, blocks, block_cols, block_count)
        if fits_columns(n_team, n_rep, features, blocks):
            return exchange_columns(n_team, n_rep, *arrays)
        return gather_and_scatter(*arrays)

    in_specs = (
        P(("team", "rep"), None),
        P(("team", "rep")),
        P("team", "rep", None, None, None),
        P("team", "rep", None),
        P("team", "rep"),
    )
    out_specs = (P(("team", "rep"), None), P(("team", "rep"), None), P(("team", "rep"), None))
    return jax.shard_map(
        on_device, mesh=mesh, in_specs=in_specs, out_specs=out_specs, check_vma=False
    )
```

```python
import functools

import jax
import jax.numpy as jnp
from jax import lax
from jax.experimental import pallas as pl
from jax.experimental.pallas import tpu as pltpu
from jax.sharding import PartitionSpec as P

HOPS = 3
PAIR = 2
LANES = 128
MESH_IDS = pl.DeviceIdType.MESH


def diffuse_kernel(n_team, n_rep, features_in, degree_in, blocks_in, cols_in, count_in,
                   out, features, degree, blocks, block_cols, block_count,
                   sent, arrived, gathered, adjacency, hops, in_sem,
                   feat_send, feat_recv, adj_send, adj_recv,
                   pass_send, pass_recv, hop_send, hop_recv, out_send, out_recv, keep_sem):
    groups = n_rep * PAIR
    chips = n_team // PAIR
    rows, width = features.shape
    group_width = width // groups
    slots, block_size = blocks.shape[2], blocks.shape[-1]
    panel = n_rep * rows
    col_blocks = n_team * rows // block_size
    team_run = n_team // col_blocks
    team, rep = lax.axis_index("team"), lax.axis_index("rep")
    chip, core = team // PAIR, lax.rem(team, PAIR)
    group = rep * PAIR + core

    loads = []
    for index, (src, dst) in enumerate(((features_in, features), (degree_in, degree),
                                        (blocks_in, blocks), (cols_in, block_cols),
                                        (count_in, block_count))):
        copy = pltpu.make_async_copy(src, dst, in_sem.at[index])
        copy.start()
        loads.append(copy)

    def column_peer(step):
        other = lax.rem(group + step, groups)
        return other, (chip * PAIR + lax.rem(other, PAIR), other // PAIR)

    def plane_peer(step):
        other = (chip + 1 - 2 * lax.rem(chip, 2), lax.rem(chip + 2, chips), chips - 1 - chip)[step - 1]
        return (other * PAIR + core, rep)

    def remote(src, dst, send_sem, recv_sem, device):
        return pltpu.make_async_remote_copy(
            src_ref=src, dst_ref=dst, send_sem=send_sem, recv_sem=recv_sem,
            device_id=device, device_id_type=MESH_IDS)

    barrier = pltpu.get_barrier_semaphore()
    for step in range(1, groups):
        pl.semaphore_signal(barrier, inc=1, device_id=column_peer(step)[1], device_id_type=MESH_IDS)
    for step in range(1, chips):
        pl.semaphore_signal(barrier, inc=1, device_id=plane_peer(step), device_id_type=MESH_IDS)

    for copy in loads:
        copy.wait()
    own_degree = degree[...].astype(jnp.float32)

    def as_column(row):
        on_diagonal = (lax.broadcasted_iota(jnp.int32, (rows, rows), 0)
                       == lax.broadcasted_iota(jnp.int32, (rows, rows), 1))
        spread = jnp.where(on_diagonal, jnp.broadcast_to(row, (rows, rows)), 0.0)
        return jnp.sum(spread, axis=1, keepdims=True)

    own_column = lax.rsqrt(as_column(own_degree))
    degree_rows = jnp.broadcast_to(jnp.concatenate(
        [own_degree, jnp.ones((1, group_width - rows), jnp.float32)], axis=1), (16, group_width))
    degree_rows = degree_rows.astype(jnp.bfloat16)
    for index in range(groups):
        part = features[:, index * group_width:(index + 1) * group_width].astype(jnp.float32)
        sent[index, 0:rows] = (own_column * part).astype(jnp.bfloat16)
        sent[index, rows:rows + 16] = degree_rows

    for column in range(col_blocks):
        dense = jnp.zeros((block_size, block_size), jnp.float32)
        for slot in range(slots):
            used = (block_cols[0, 0, slot] == column) & (slot < block_count[0, 0])
            factor = jnp.where(used, 1.0, 0.0).astype(jnp.float32)
            dense = dense + factor * blocks[0, 0, slot].astype(jnp.float32)
        adjacency[rep, core, column] = dense.astype(jnp.bfloat16)

    pl.semaphore_wait(barrier, groups - 1 + chips - 1)

    feature_copies, adjacency_copies, pass_copies = [], [], []
    for step in range(1, groups):
        other, device = column_peer(step)
        copy = remote(sent.at[other], arrived.at[rep, core],
                      feat_send.at[step - 1], feat_recv.at[step - 1], device)
        copy.start()
        feature_copies.append(copy)

    def adjacency_of(which):
        return adjacency.at[which, core]

    sibling = (chip * PAIR + lax.rem(core + 1, PAIR), rep)
    for step in range(1, n_rep):
        copy = remote(adjacency_of(rep), adjacency_of(rep),
                      adj_send.at[step - 1], adj_recv.at[step - 1],
                      (team, lax.rem(rep + step, n_rep)))
        copy.start()
        adjacency_copies.append(copy)
    copy = remote(adjacency_of(rep), adjacency_of(rep), pass_send.at[0], pass_recv.at[0], sibling)
    copy.start()
    pass_copies.append(copy)
    arrived[rep, core] = sent[group]

    panels = (lax.rem(core + 1, PAIR), core)

    def send_hop(hop, half):
        copies = []
        own = gathered.at[hop, :, chip * PAIR + panels[half]]
        for step in (3, 1, 2):
            copy = remote(own, own, hop_send.at[hop, half, step - 1],
                          hop_recv.at[hop, half, step - 1], plane_peer(step))
            copy.start()
            copies.append(copy)
        return [copies[1], copies[0], copies[2]]

    for copy in feature_copies:
        copy.wait_recv()
    for c in range(PAIR):
        gathered[0, :, chip * PAIR + c] = arrived[:, c, 0:rows]
    hop_copies = [[send_hop(0, half) for half in range(PAIR)]]

    for step in range(1, n_rep):
        adjacency_copies[step - 1].wait_recv()
        source = lax.rem(rep + n_rep - step, n_rep)
        copy = remote(adjacency_of(source), adjacency_of(source),
                      pass_send.at[step], pass_recv.at[step], sibling)
        copy.start()
        pass_copies.append(copy)
    scale_columns = [
        lax.rsqrt(jnp.concatenate(
            [as_column(arrived[r, c, rows:rows + 16].astype(jnp.float32)[0:1, 0:rows])
             for r in range(n_rep)], axis=0))
        for c in panels]

    near = team // team_run
    mine = pl.ds(pl.multiple_of(group * group_width, LANES), group_width)

    def product(hop, column, c):
        piece = gathered[hop, :, pl.ds(column * team_run, team_run)]
        weights = jnp.concatenate([adjacency[r, c, column] for r in range(n_rep)], axis=1)
        return jnp.dot(weights, piece.reshape(n_rep * block_size, group_width),
                       preferred_element_type=jnp.float32)

    out_copies, kept_copies = [], []
    for hop in range(HOPS):
        for copies in hop_copies[hop]:
            copies[0].wait_recv()
        totals = [gathered[hop, :, chip * PAIR + c].reshape(panel, group_width).astype(jnp.float32)
                  for c in panels]
        if hop == 0:
            for copies in hop_copies[hop]:
                for copy in copies[1:]:
                    copy.wait_recv()
            for step in range(n_rep):
                pass_copies[step].wait_recv()
                source = lax.rem(rep + n_rep - step, n_rep)
                piece = gathered[hop, source].reshape(col_blocks * block_size, group_width)
                for half, c in enumerate(panels):
                    weights = jnp.concatenate(
                        [adjacency[source, c, column] for column in range(col_blocks)], axis=1)
                    totals[half] = totals[half] + jnp.dot(
                        weights, piece, preferred_element_type=jnp.float32)
        else:
            for half, c in enumerate(panels):
                totals[half] = totals[half] + product(hop, near, c)
            for copies in hop_copies[hop]:
                for copy in copies[1:]:
                    copy.wait_recv()
        if hop < HOPS - 1:
            hop_copies.append([])
        for half, c in enumerate(panels):
            total = totals[half]
            if hop > 0:
                total = total + product(hop, col_blocks - 1 - near, c)
            current = (scale_columns[half] * total).astype(jnp.bfloat16)
            if hop < HOPS - 1:
                following = (scale_columns[half] * current.astype(jnp.float32)).astype(jnp.bfloat16)
                gathered[hop + 1, :, chip * PAIR + c] = following.reshape(n_rep, rows, group_width)
                hop_copies[hop + 1].append(send_hop(hop + 1, half))
            hops[hop, c] = current.reshape(n_rep, rows, group_width)
            part = {HOPS - 2: (0, HOPS - 1), HOPS - 1: (HOPS - 1, 1)}.get(hop)
            if part is None:
                continue
            share = pl.ds(*part)
            which = hop - (HOPS - 2)
            for step in range(1, groups):
                if step % PAIR == 1 - half:
                    other, device = column_peer(step)
                    copy = remote(hops.at[share, c, other // PAIR], out.at[share, :, mine],
                                  out_send.at[which, step - 1], out_recv.at[which, step - 1], device)
                    copy.start()
                    out_copies.append(copy)
            if half == PAIR - 1:
                kept = pltpu.make_async_copy(hops.at[share, core, rep], out.at[share, :, mine],
                                             keep_sem.at[which])
                kept.start()
                kept_copies.append(kept)

    for copy in out_copies:
        copy.wait_recv()
    for copy in kept_copies:
        copy.wait()
    for copies in [feature_copies, adjacency_copies, pass_copies, out_copies]:
        for copy in copies:
            copy.wait_send()
    for halves in hop_copies:
        for copies in halves:
            for copy in copies:
                copy.wait_send()


def store_kernel(results, out1, out2, out3, held, load_sem, store_sem):
    refs = tuple((results.at[index], out) for index, out in enumerate((out1, out2, out3)))
    loads = [pltpu.make_async_copy(src, held.at[index], load_sem.at[index])
             for index, (src, dst) in enumerate(refs)]
    stores = [pltpu.make_async_copy(held.at[index], dst, store_sem.at[index])
              for index, (src, dst) in enumerate(refs)]
    for load in loads:
        load.start()
    for load, store in zip(loads, stores):
        load.wait()
        store.start()
    for store in stores:
        store.wait()


def exchange_columns(n_team, n_rep, features, degree, blocks, block_cols, block_count):
    rows, width = features.shape
    groups = n_rep * PAIR
    chips = n_team // PAIR
    group_width = width // groups
    panel = n_rep * rows
    col_blocks = n_team * rows // panel
    dma = pltpu.SemaphoreType.DMA
    hbm = pl.BlockSpec(memory_space=pltpu.HBM)
    result = jax.ShapeDtypeStruct((rows, width), jnp.bfloat16)
    results = pl.pallas_call(
        functools.partial(diffuse_kernel, n_team, n_rep),
        out_shape=jax.ShapeDtypeStruct((HOPS, rows, width), jnp.bfloat16),
        in_specs=[hbm] * 5,
        out_specs=hbm,
        scratch_shapes=[
            pltpu.VMEM((rows, width), jnp.bfloat16),
            pltpu.VMEM((1, rows), jnp.int32),
            pltpu.VMEM(blocks.shape, jnp.bfloat16),
            pltpu.SMEM(block_cols.shape, jnp.int32),
            pltpu.SMEM(block_count.shape, jnp.int32),
            pltpu.VMEM((groups, rows + 16, group_width), jnp.bfloat16),
            pltpu.VMEM((n_rep, PAIR, rows + 16, group_width), jnp.bfloat16),
            pltpu.VMEM((HOPS, n_rep, n_team, rows, group_width), jnp.bfloat16),
            pltpu.VMEM((n_rep, PAIR, col_blocks, panel, panel), jnp.bfloat16),
            pltpu.VMEM((HOPS, PAIR, n_rep, rows, group_width), jnp.bfloat16),
            dma((5,)),
            dma((groups - 1,)), dma((groups - 1,)),
            dma((n_rep - 1,)), dma((n_rep - 1,)),
            dma((n_rep,)), dma((n_rep,)),
            dma((HOPS, PAIR, chips - 1)), dma((HOPS, PAIR, chips - 1)),
            dma((2, groups - 1)), dma((2, groups - 1)),
            dma((2,)),
        ],
        compiler_params=pltpu.CompilerParams(
            collective_id=0, has_side_effects=True, vmem_limit_bytes=62 * 1024 * 1024),
    )(features, degree[None, :], blocks, block_cols, block_count)
    return pl.pallas_call(
        store_kernel,
        out_shape=(result,) * HOPS,
        in_specs=[hbm],
        out_specs=(hbm,) * HOPS,
        scratch_shapes=[pltpu.VMEM((HOPS, rows, width), jnp.bfloat16), dma((HOPS,)), dma((HOPS,))],
        compiler_params=pltpu.CompilerParams(vmem_limit_bytes=62 * 1024 * 1024),
    )(results)


def gather_and_scatter(features, degree, blocks, block_cols, block_count):
    width = features.shape[1]
    block_size = blocks.shape[-1]
    row_blocks = blocks.shape[0]
    col_blocks = blocks.shape[2]
    panel = row_blocks * block_size
    tiles = blocks[:, 0]
    columns_used = block_cols[:, 0]
    counts_used = block_count[:, 0]
    scale = lax.rsqrt(degree.astype(jnp.float32))[:, None]
    current = features
    results = []
    for hop in range(HOPS):
        sent = (scale * current.astype(jnp.float32)).astype(jnp.bfloat16)
        whole = lax.all_gather(sent, "team", axis=0, tiled=True)
        pieces = whole.reshape(col_blocks, block_size, width)

        def row_block(which, accum):

            def add_slot(slot, inner):
                tile = tiles[which, slot]
                piece = pieces[columns_used[which, slot]]
                return inner + jnp.dot(tile, piece, preferred_element_type=jnp.float32)

            block_rows = lax.fori_loop(
                0, counts_used[which], add_slot, jnp.zeros((block_size, width), jnp.float32)
            )
            return lax.dynamic_update_slice_in_dim(accum, block_rows, which * block_size, 0)

        partial_value = lax.fori_loop(
            0, row_blocks, row_block, jnp.zeros((panel, width), jnp.float32)
        )
        total = lax.psum_scatter(
            partial_value.astype(jnp.bfloat16), "rep", scatter_dimension=0, tiled=True
        ).astype(jnp.float32)
        current = (scale * (total + sent.astype(jnp.float32))).astype(jnp.bfloat16)
        results.append(current)
    return (results[0], results[1], results[2])


def fits_columns(n_team, n_rep, features, blocks):
    rows, width = features.shape
    return (width % (n_rep * PAIR * LANES) == 0 and n_team == 4 * PAIR
            and n_team * rows == 2 * blocks.shape[-1]
            and n_rep > 1 and blocks.shape[0] == 1 and rows % 16 == 0 and rows < LANES
            and blocks.shape[-1] == n_rep * rows
            and blocks.shape[-1] % LANES == 0
            and n_rep * n_team * rows * n_rep * rows * 4 <= 4 * 1024 * 1024)


def solution(mesh):
    n_team, n_rep = mesh.shape["team"], mesh.shape["rep"]

    def on_device(features, degree, blocks, block_cols, block_count):
        arrays = (features, degree, blocks, block_cols, block_count)
        if fits_columns(n_team, n_rep, features, blocks):
            return exchange_columns(n_team, n_rep, *arrays)
        return gather_and_scatter(*arrays)

    in_specs = (
        P(("team", "rep"), None),
        P(("team", "rep")),
        P("team", "rep", None, None, None),
        P("team", "rep", None),
        P("team", "rep"),
    )
    out_specs = (P(("team", "rep"), None), P(("team", "rep"), None), P(("team", "rep"), None))
    return jax.shard_map(
        on_device, mesh=mesh, in_specs=in_specs, out_specs=out_specs, check_vma=False
    )
```
